32 devices in a mesh: groups: 2 (over y), ctx: 4 (over z), head: 2 (over x), row: 2 (over core).
Axes of the slice: x: 2, y: 2, z: 4, core: 2. Of those that a mesh axis runs over, the one named last changes fastest.
Arguments:
- queries: bfloat16 [512, 4, 8192], P(('groups', 'ctx', 'row'), None, 'head'), parts along dimension 0, may hold values from -128 to 128
- row_new_keys: bfloat16 [512, 4, 1024], P(('groups', 'ctx', 'row'), None, 'head'), parts along dimension 0, may hold values from -4 to 4
- row_new_values: bfloat16 [512, 4, 1024], P(('groups', 'ctx', 'row'), None, 'head'), parts along dimension 0, may hold values from -6 to 6
- prefix_page_keys: bfloat16 [4096, 1024], P(('groups', 'ctx'), 'head'), parts along dimension 0, may hold values from -6 to 6
- prefix_page_values: bfloat16 [4096, 1024], P(('groups', 'ctx'), 'head'), parts along dimension 0, may hold values from -6 to 6
- block_pages: int32 [64, 8], P('groups'), parts along dimension 0, may hold values from 0 to 15, as said below
- row_len: int32 [512], P(('groups', 'ctx', 'row')), parts along dimension 0, may hold values from 1 to 8
- home: int32 [512, 1], P(('groups', 'ctx', 'row')), parts along dimension 0, may hold values from 0 to 7; in each aligned block of 32 rows (0 to 31, 32 to 63, ...) at most 8 rows name the same one
Outputs:
- delivered: bfloat16 [16, 8, 8, 4, 8192], P(('groups', 'ctx', 'row'), None, None, None, 'head'), parts along dimension 0
The draws below stay inside these ranges and needn't reach their ends.
There are 2 independent parts, one for each index of `groups`. The reference program is written for one: setup_inputs(seed, part) draws one part's arguments, and reference() takes and returns one part's arrays. A program takes and returns all parts, laid end to end along the dimension named above; each array names one. Nothing has to cross between parts.
Inputs may be any that keep to these rules, and one draw needn't show every extreme that they name: `block_pages`: each row block's entries are distinct pages; blocks 2i and 2i + 1 share their first half of entries. `home`: among the 32 rows of one device, at most 8 name the same owner.
All inputs are finite; a program needn't handle non-finite values.
Results may differ from the reference program's by a relative error of at most 0.0055.
Values may be sent and summed in bfloat16 or wider, within the bound.
A program may use at most 64 MiB of HBM per device.

```python
import math
import jax
import jax.numpy as jnp
import numpy as np
from jax import lax

QUERY_HEADS = 64
KEY_HEADS = 8
HEAD_SIZE = 128
NEW_TOKENS = 4
PAGE_TOKENS = 128
BLOCK_ROWS = 8
ROW_DEV = 32
QUERY_PER_KEY = 8
OWNERS = 8
SEND_CAP = 8
QUERY_ROWS = 256
BLOCKS = 32
POOL = 16
PREFIX_TOKENS = 2048
SLOTS = 8


def shared_keys(key):
    return jnp.clip(jax.random.normal(key, (QUERY_ROWS, NEW_TOKENS, KEY_HEADS * HEAD_SIZE), jnp.float32), -4.0, 4.0)


def draw_queries(key, part):
    key = jax.random.fold_in(key, 3)
    return jnp.clip(jax.random.normal(key, (QUERY_ROWS, NEW_TOKENS, QUERY_HEADS * HEAD_SIZE), jnp.float32), -4.0, 4.0).astype(jnp.bfloat16)


def draw_row_new_keys(key, part):
    common_prefix = shared_keys(key)
    return common_prefix.astype(jnp.bfloat16)


def one_order(subkey):
    return jax.random.permutation(subkey, POOL)


def draw_block_pages(key, part):
    key = jax.random.fold_in(key, 7)
    pair_count = BLOCKS // 2
    orders = jax.vmap(one_order)(jax.random.split(key, pair_count))
    half_slots = SLOTS // 2
    first_table = orders[:, :SLOTS]
    second_table = jnp.concatenate([orders[:, :half_slots], orders[:, SLOTS:SLOTS + half_slots]], axis=1)
    return jnp.stack([first_table, second_table], axis=1).reshape(BLOCKS, SLOTS).astype(jnp.int32)


def with_ends(array, key, low, largest):
    index_at = [jax.random.randint(jax.random.fold_in(key, axis), (), 0, length) for axis, length in enumerate(array.shape)]
    main_axis = array.shape.index(max(array.shape))
    beside = index_at[:main_axis] + [(index_at[main_axis] + 1) % array.shape[main_axis]] + index_at[main_axis + 1:]
    return array.at[tuple(index_at)].set(low).at[tuple(beside)].set(largest)


def block_scale(key, extent, cuts, least, high):
    level, own = 1.0, jax.random.fold_in(key, 6)
    for dim, parts in cuts:
        steps = jnp.exp(jax.random.uniform(jax.random.fold_in(own, dim), (parts,), jnp.float32, least / len(cuts), high / len(cuts)))
        level = level * jnp.repeat(steps, extent[dim] // parts).reshape([-1 if axis == dim else 1 for axis in range(len(extent))])
    return level


def routed_block(key, own, number, rows, number_of, top, reach, skew):
    order = jax.random.permutation(key, number_of)
    packed, usual = shares(number_of, rows * top, reach, skew, True), shares(number_of, rows * top, reach, skew, False)
    places = jnp.arange(number_of)

    def named(sizes, turn):
        used = int((sizes > 0).sum())
        fixed = max(1, used // 4)
        shifted = fixed + (places - fixed + turn * (used - fixed)) % max(1, number_of - fixed)
        return jnp.zeros((number_of,), jnp.int32).at[order[jnp.where(places < fixed, places, shifted)]].set(jnp.asarray(sizes, jnp.int32))

    sizes = jnp.where(number % 4 == 0, named(packed, number // 4), named(usual, number - number // 4 - 1))
    mixed = jax.random.permutation(jax.random.fold_in(own, 3), number_of)
    source_of, taker = mixed[0:number_of // 2 * 2:2], mixed[1:number_of // 2 * 2:2]
    room = jnp.minimum(sizes[source_of] - 1, reach - sizes[taker]) // 2
    room = jnp.where((source_of == order[0]) | (taker == order[0]) | (sizes[taker] == 0), 0, jnp.maximum(room, 0))
    shifted = jax.random.randint(jax.random.fold_in(own, 4), (number_of // 2,), 0, 1 << 20) % (room + 1)
    sizes = sizes.at[source_of].add(-shifted).at[taker].add(shifted)
    labels = jnp.searchsorted(jnp.cumsum(sizes), jnp.arange(rows * top), side="right").astype(jnp.int32)
    grid = labels.reshape(top, rows).T
    grid = grid[jax.random.permutation(jax.random.fold_in(own, 1), rows)]
    turn = jax.random.randint(jax.random.fold_in(own, 2), (rows, 1), 0, top)
    return jnp.take_along_axis(grid, (jnp.arange(top)[None, :] + turn) % top, axis=1)


def shares(number_of, total, most, skew, full):
    weights = [(1 << 20) // math.isqrt(standing ** skew) + 1 for standing in range(1, number_of + 1)]
    largest = most if full else min(most, max(-(-total // number_of), total * weights[0] // sum(weights)))
    least = 1 if total - largest >= number_of - 1 else 0
    holding, surplus = [largest] + [least] * (number_of - 1), total - largest - least * (number_of - 1)
    while surplus > 0:
        candidates = [i for i in range(1, number_of) if holding[i] < largest] or [i for i in range(1, number_of) if holding[i] < most]
        whole, left = sum([weights[i] for i in candidates]), surplus
        for i in candidates:
            more = min(most - holding[i], max(1, left * weights[i] // whole), surplus)
            holding[i] = holding[i] + more
            surplus = surplus - more
    return np.array(holding)


def scatter_about(key, shape, width, limit, pieces=(), kind=jnp.bfloat16):
    gain = block_scale(key, shape, pieces, -0.22, 0.18) if pieces else 1.0
    entries = jax.random.normal(key, shape, jnp.float32) * width * gain
    return jnp.minimum(jnp.maximum(entries, -limit), limit).astype(kind)


def setup_inputs(seed: int = 0, part: int = 0) -> dict:
    streams_of = jax.random.split(jax.random.key(seed), 9)
    own_keys = jax.random.split(jax.random.fold_in(streams_of[8], part), 9)
    queries = draw_queries(jax.random.fold_in(jax.random.fold_in(streams_of[8], part), 71), part)
    row_new_keys = draw_row_new_keys(jax.random.fold_in(jax.random.fold_in(streams_of[8], part), 71), part)
    row_new_values = scatter_about(own_keys[2], (QUERY_ROWS, NEW_TOKENS, KEY_HEADS * HEAD_SIZE), 1.0, 6.0, ((0, 8), (2, 2)))
    prefix_page_keys = scatter_about(own_keys[3], (PREFIX_TOKENS, KEY_HEADS * HEAD_SIZE), 1.0, 6.0, ((0, 4), (1, 2)))
    prefix_page_values = scatter_about(own_keys[4], (PREFIX_TOKENS, KEY_HEADS * HEAD_SIZE), 1.0, 6.0, ((0, 4), (1, 2)))
    block_pages = draw_block_pages(jax.random.fold_in(jax.random.fold_in(streams_of[8], part), 71), part)
    row_len = with_ends(jax.random.randint(own_keys[6], (QUERY_ROWS,), 1, SLOTS + 1), jax.random.fold_in(own_keys[6], 1), 1, SLOTS).astype(jnp.int32)
    home_keys = jax.random.split(jax.random.fold_in(own_keys[7], 1), QUERY_ROWS // ROW_DEV)
    home_turns = jax.random.permutation(jax.random.fold_in(own_keys[7], 3), QUERY_ROWS // ROW_DEV)
    home = jax.vmap(lambda own, number: routed_block(jax.random.fold_in(own_keys[7], 2), own, number, ROW_DEV, OWNERS, 1, SEND_CAP, 1))(home_keys, home_turns).reshape((QUERY_ROWS, 1))
    return dict(queries=queries, row_new_keys=row_new_keys, row_new_values=row_new_values, prefix_page_keys=prefix_page_keys, prefix_page_values=prefix_page_values, block_pages=block_pages, row_len=row_len, home=home)


LOWEST = -1.0e30


def reference(queries, row_new_keys, row_new_values, prefix_page_keys, prefix_page_values, block_pages, row_len, home):
    factor = HEAD_SIZE ** -0.5
    prefix_pool_pages = prefix_page_keys.shape[0] // PAGE_TOKENS
    paged_key_rows = prefix_page_keys.reshape(prefix_pool_pages, PAGE_TOKENS, KEY_HEADS, HEAD_SIZE)
    paged_value_rows = prefix_page_values.reshape(prefix_pool_pages, PAGE_TOKENS, KEY_HEADS, HEAD_SIZE)
    causal = (jnp.arange(NEW_TOKENS)[None, :] <= jnp.arange(NEW_TOKENS)[:, None])[None, :, None, None, :]

    def one_block(number):
        leading_row = (number * BLOCK_ROWS).astype(jnp.int32)
        grouped_heads = lax.dynamic_slice_in_dim(queries, leading_row, BLOCK_ROWS, 0).astype(jnp.float32)
        grouped_heads = grouped_heads.reshape(BLOCK_ROWS, NEW_TOKENS, KEY_HEADS, QUERY_PER_KEY, HEAD_SIZE)
        fresh_keys = lax.dynamic_slice_in_dim(row_new_keys, leading_row, BLOCK_ROWS, 0).astype(jnp.float32).reshape(BLOCK_ROWS, NEW_TOKENS, KEY_HEADS, HEAD_SIZE)
        fresh_values = lax.dynamic_slice_in_dim(row_new_values, leading_row, BLOCK_ROWS, 0).astype(jnp.float32).reshape(BLOCK_ROWS, NEW_TOKENS, KEY_HEADS, HEAD_SIZE)
        table = lax.dynamic_index_in_dim(block_pages, number.astype(jnp.int32), 0, keepdims=False)
        lengths = lax.dynamic_slice_in_dim(row_len, leading_row, BLOCK_ROWS, 0)
        keys_old = jnp.take(paged_key_rows, table, axis=0).astype(jnp.float32)
        values_old = jnp.take(paged_value_rows, table, axis=0).astype(jnp.float32)
        old_scores = jnp.einsum("rtjgd,spjd->rtjgsp", grouped_heads, keys_old) * factor
        new_scores = jnp.einsum("rtjgd,rujd->rtjgu", grouped_heads, fresh_keys) * factor
        live_slots = (jnp.arange(SLOTS)[None, :] < lengths[:, None])[:, None, None, None, :, None]
        peak = jnp.maximum(jnp.max(jnp.where(live_slots, old_scores, LOWEST), axis=(4, 5)),
                           jnp.max(jnp.where(causal, new_scores, LOWEST), axis=4))
        weight_old = jnp.where(live_slots, jnp.exp(old_scores - peak[..., None, None]), 0.0)
        weight_new = jnp.where(causal, jnp.exp(new_scores - peak[..., None]), 0.0)
        totals = jnp.sum(weight_old, axis=(4, 5)) + jnp.sum(weight_new, axis=4)
        rounded_old = lax.optimization_barrier(weight_old.astype(jnp.bfloat16)).astype(jnp.float32)
        rounded_new = lax.optimization_barrier(weight_new.astype(jnp.bfloat16)).astype(jnp.float32)
        weighted = jnp.einsum("rtjgsp,spjd->rtjgd", rounded_old, values_old)
        weighted = weighted + jnp.einsum("rtjgu,rujd->rtjgd", rounded_new, fresh_values)
        return (weighted / totals[..., None]).astype(jnp.bfloat16).reshape(BLOCK_ROWS, NEW_TOKENS, QUERY_HEADS * HEAD_SIZE)

    attended = lax.map(one_block, jnp.arange(BLOCKS, dtype=jnp.int32)).reshape(QUERY_ROWS, NEW_TOKENS, QUERY_HEADS * HEAD_SIZE)
    targets = home[:, 0].reshape(OWNERS, ROW_DEV)
    row_order = jnp.arange(ROW_DEV)
    earlier = (targets[:, :, None] == targets[:, None, :]) & (row_order[:, None] > row_order[None, :])[None, :, :]
    position = jnp.sum(earlier.astype(jnp.int32), axis=2)
    source = jnp.arange(OWNERS, dtype=jnp.int32)[:, None]
    destination = ((targets * OWNERS + source) * SEND_CAP + position).reshape(-1).astype(jnp.int32)
    delivered = jnp.zeros((OWNERS * OWNERS * SEND_CAP, NEW_TOKENS, QUERY_HEADS * HEAD_SIZE), jnp.bfloat16)
    delivered = delivered.at[destination].set(attended)
    return delivered.reshape(OWNERS, OWNERS, SEND_CAP, NEW_TOKENS, QUERY_HEADS * HEAD_SIZE)
```

```python
import functools

import jax
import jax.numpy as jnp
from jax import lax
from jax.experimental import pallas as pl
from jax.experimental.pallas import tpu as pltpu
from jax.sharding import PartitionSpec as P

HEAD_SIZE = 128
PAGE_TOKENS = 128
BLOCK_ROWS = 8
LOWEST = -1e30
STACK = 2
MESH = pl.DeviceIdType.MESH


def kernel(
    dims,
    len_ref,
    home_ref,
    pages_ref,
    q_ref,
    nk_ref,
    nv_ref,
    pk_ref,
    pv_ref,
    out_ref,
    kv,
    bias,
    own_bias,
    scores,
    own_scores,
    placing,
    outbox,
    load_sem,
    up_send,
    down_send,
    z_recv,
    mate_send,
    mate_recv,
    out_send,
    out_recv,
    own_sem,
):
    ctx, steps, cap, kv_heads, per_key = dims
    rows4 = q_ref.shape[0]
    rows = rows4 // steps
    owners = 2 * ctx
    half = kv.shape[4]
    slots = pages_ref.shape[1]
    pool = ctx * 2 * half // PAGE_TOKENS
    wide = per_key * HEAD_SIZE
    pieces = 2 * ctx
    c = lax.axis_index("ctx")
    r = lax.axis_index("row")
    me = c * 2 + r
    factor = HEAD_SIZE ** (-0.5)

    def load(j, h, which):
        source = (pk_ref, pv_ref)[which]
        return pltpu.make_async_copy(
            source.at[pl.ds(h * half, half), pl.ds(j * HEAD_SIZE, HEAD_SIZE)],
            kv.at[j, c, h, which],
            load_sem.at[j, h, which],
        )

    for j in range(kv_heads):
        for h in range(2):
            for which in range(2):
                load(j, h, which).start()

    barrier = pltpu.get_barrier_semaphore()

    def greet(k, _):
        other = lax.rem(me + k, owners)
        pl.semaphore_signal(
            barrier,
            inc=1,
            device_id={"ctx": other // 2, "row": lax.rem(other, 2)},
            device_id_type=MESH,
        )
        return 0

    lax.fori_loop(1, owners, greet, 0)
    pl.semaphore_wait(barrier, owners - 1)

    def along(j, o, ahead):
        step = 1 if ahead else -1
        target = jnp.clip(c + step, 0, ctx - 1)
        return pltpu.make_async_remote_copy(
            src_ref=kv.at[j, o, r],
            dst_ref=kv.at[j, o, r],
            send_sem=(up_send if ahead else down_send).at[j, o],
            recv_sem=z_recv.at[j, o],
            device_id={"ctx": target, "row": r},
            device_id_type=MESH,
        )

    def across(j, o, h):
        return pltpu.make_async_remote_copy(
            src_ref=kv.at[j, o, h],
            dst_ref=kv.at[j, o, h],
            send_sem=mate_send.at[j, o],
            recv_sem=mate_recv.at[j, o],
            device_id={"ctx": c, "row": 1 - r},
            device_id_type=MESH,
        )

    def send_own(j):
        @pl.when(c < ctx - 1)
        def _():
            along(j, c, True).start()

        @pl.when(c > 0)
        def _():
            along(j, c, False).start()

    def relay(j, s):
        low, high = c - s, c + s

        @pl.when(low >= 0)
        def _():
            along(j, low, True).wait_recv()

            @pl.when(c < ctx - 1)
            def _():
                along(j, low, True).start()

            across(j, low, r).start()

        @pl.when(high < ctx)
        def _():
            along(j, high, False).wait_recv()

            @pl.when(c > 0)
            def _():
                along(j, high, False).start()

            across(j, high, r).start()

    def wait_mate(j):
        def one(k, _):
            o = lax.rem(c + k, ctx)
            across(j, o, 1 - r).wait_recv()
            return 0

        lax.fori_loop(1, ctx, one, 0)

    for j in range(kv_heads):
        for h in range(2):
            for which in range(2):
                load(j, h, which).wait()
        send_own(j)

    row_of = lax.broadcasted_iota(jnp.int32, (rows4, 1), 0) // steps
    lane_row = lax.broadcasted_iota(jnp.int32, (1, rows4), 1) // steps
    lane_step = lax.rem(lax.broadcasted_iota(jnp.int32, (1, rows4), 1), steps)
    length = jnp.zeros((rows4, 1), jnp.int32)
    home_col = jnp.zeros((rows4, 1), jnp.int32)
    home_lane = jnp.zeros((1, rows4), jnp.int32)
    for i in range(rows):
        length = jnp.where(row_of == i, len_ref[i], length)
        home_col = jnp.where(row_of == i, home_ref[i], home_col)
        home_lane = jnp.where(lane_row == i, home_ref[i], home_lane)

    page_id = lax.broadcasted_iota(jnp.int32, (rows4, pool), 1)
    used = jnp.zeros((rows4, pool), jnp.float32)
    block_of = row_of // BLOCK_ROWS
    first_block = me * (rows // BLOCK_ROWS)
    for slot in range(slots):
        page = jnp.zeros((rows4, 1), jnp.int32)
        for b in range(rows // BLOCK_ROWS):
            page = jnp.where(block_of == b, pages_ref[first_block + b, slot], page)
        page = jnp.where(slot < length, page, -1)
        used = jnp.where(page_id == page, 1.0, used)
    floor = jnp.where(used > 0.5, 0.0, LOWEST)
    per_piece = half // PAGE_TOKENS
    for p in range(pool):
        at = (p % per_piece) * PAGE_TOKENS
        bias[p // per_piece, :, at : at + PAGE_TOKENS] = jnp.broadcast_to(
            floor[:, p : p + 1], (rows4, PAGE_TOKENS)
        )
    row_step = lax.rem(lax.broadcasted_iota(jnp.int32, (rows4, 1), 0), steps)
    own_bias[...] = jnp.where((row_of == lane_row) & (lane_step <= row_step), 0.0, LOWEST)

    earlier = (home_col == home_lane) & (row_of < lane_row) & (row_step == 0)
    position = jnp.sum(jnp.where(earlier, 1.0, 0.0), axis=0, keepdims=True).astype(jnp.int32)
    target = (home_lane * cap + position) * steps + lane_step
    slot_row = lax.broadcasted_iota(jnp.int32, (owners * cap * steps, rows4), 0)
    placing[...] = jnp.where(slot_row == target, 1.0, 0.0).astype(jnp.bfloat16)

    def first(s, _):
        relay(0, s)
        return 0

    lax.fori_loop(1, ctx, first, 0)

    chunks = per_key // STACK
    relays = -(-(ctx - 1) // chunks)
    contract = (((1,), (1,)), ((), ()))

    def over_pieces(step, init):
        if pieces <= 8:
            state = init
            for i in range(pieces):
                state = step(i, i // 2, i % 2, state)
            return state
        return lax.fori_loop(0, pieces, lambda i, st: step(i, i // 2, lax.rem(i, 2), st), init)

    def fold(op, array):
        got = array[:, :HEAD_SIZE]
        for at in range(HEAD_SIZE, array.shape[1], HEAD_SIZE):
            got = op(got, array[:, at : at + HEAD_SIZE])
        return got

    def send_result(j, o):
        return pltpu.make_async_remote_copy(
            src_ref=outbox.at[j, o],
            dst_ref=out_ref.at[me, :, pl.ds(pl.multiple_of(j * wide, wide), wide)],
            send_sem=out_send.at[j, o],
            recv_sem=out_recv.at[j, me],
            device_id={"ctx": o // 2, "row": lax.rem(o, 2)},
            device_id_type=MESH,
        )

    def take_result(j, o):
        return pltpu.make_async_remote_copy(
            src_ref=outbox.at[j, o],
            dst_ref=out_ref.at[o, :, pl.ds(pl.multiple_of(j * wide, wide), wide)],
            send_sem=out_send.at[j, o],
            recv_sem=out_recv.at[j, o],
            device_id={"ctx": o // 2, "row": lax.rem(o, 2)},
            device_id_type=MESH,
        )

    def keep_result(j):
        return pltpu.make_async_copy(
            outbox.at[j, me],
            out_ref.at[me, :, pl.ds(pl.multiple_of(j * wide, wide), wide)],
            own_sem.at[j],
        )

    def one_head(j, _):
        wait_mate(j)
        head_at = pl.multiple_of(j * HEAD_SIZE, HEAD_SIZE)

        def one_chunk(k, _):
            @pl.when(j + 1 < kv_heads)
            def _():
                for i in range(relays):
                    s = k * relays + i + 1

                    @pl.when(s < ctx)
                    def _():
                        relay(j + 1, s)

            lead = (j * per_key + k * STACK) * HEAD_SIZE
            query = jnp.concatenate(
                [
                    q_ref[:, pl.ds(pl.multiple_of(lead + g * HEAD_SIZE, HEAD_SIZE), HEAD_SIZE)]
                    for g in range(STACK)
                ],
                axis=0,
            )
            own = (
                lax.dot_general(
                    query,
                    nk_ref[:, pl.ds(head_at, HEAD_SIZE)],
                    contract,
                    preferred_element_type=jnp.float32,
                )
                * factor
                + jnp.concatenate([own_bias[...]] * STACK, axis=0)
            )

            def score(i, o, h, peak):
                got = (
                    lax.dot_general(
                        query, kv[j, o, h, 0], contract, preferred_element_type=jnp.float32
                    )
                    * factor
                    + jnp.concatenate([bias[i]] * STACK, axis=0)
                )
                scores[i] = got
                return jnp.maximum(peak, fold(jnp.maximum, got))

            peak = jnp.max(over_pieces(score, own), axis=1, keepdims=True)
            weight = jnp.exp(own - peak)
            total = weight
            summed = jnp.dot(
                weight.astype(jnp.bfloat16),
                nv_ref[:, pl.ds(head_at, HEAD_SIZE)],
                preferred_element_type=jnp.float32,
            )

            def gather(i, o, h, state):
                total, summed = state
                weight = jnp.exp(scores[i] - peak)
                summed = summed + jnp.dot(
                    weight.astype(jnp.bfloat16), kv[j, o, h, 1], preferred_element_type=jnp.float32
                )
                return total + fold(jnp.add, weight), summed

            total, summed = over_pieces(gather, (total, summed))
            attended = (summed / jnp.sum(total, axis=1, keepdims=True)).astype(jnp.bfloat16)
            for g in range(STACK):
                placed = jnp.dot(
                    placing[...],
                    attended[g * rows4 : (g + 1) * rows4],
                    preferred_element_type=jnp.float32,
                )
                at = pl.multiple_of((k * STACK + g) * HEAD_SIZE, HEAD_SIZE)
                outbox[j, :, :, pl.ds(at, HEAD_SIZE)] = placed.reshape(
                    owners, cap * steps, HEAD_SIZE
                ).astype(jnp.bfloat16)
            return 0

        lax.fori_loop(0, chunks, one_chunk, 0)

        def deliver(k, _):
            send_result(j, lax.rem(me + k, owners)).start()
            return 0

        lax.fori_loop(1, owners, deliver, 0)
        keep_result(j).start()
        return 0

    lax.fori_loop(0, kv_heads, one_head, 0)

    def settle(j, _):
        keep_result(j).wait()

        def pages(k, _):
            o = lax.rem(c + k, ctx)
            across(j, o, r).wait_send()
            return 0

        lax.fori_loop(1, ctx, pages, 0)

        def hops(o, _):
            @pl.when((c < ctx - 1) & (o <= c))
            def _():
                along(j, o, True).wait_send()

            @pl.when((c > 0) & (o >= c))
            def _():
                along(j, o, False).wait_send()

            return 0

        lax.fori_loop(0, ctx, hops, 0)

        def results(k, _):
            o = lax.rem(me + k, owners)
            send_result(j, o).wait_send()
            take_result(j, o).wait_recv()
            return 0

        lax.fori_loop(1, owners, results, 0)
        return 0

    lax.fori_loop(0, kv_heads, settle, 0)


def body(
    queries,
    row_new_keys,
    row_new_values,
    prefix_page_keys,
    prefix_page_values,
    block_pages,
    row_len,
    home,
):
    rows, steps, width = queries.shape
    kv_heads = row_new_keys.shape[2] // HEAD_SIZE
    per_key = width // row_new_keys.shape[2]
    ctx = lax.axis_size("ctx")
    owners = ctx * lax.axis_size("row")
    cap = max(2, 2 * rows // owners)
    tokens = prefix_page_keys.shape[0]
    half = tokens // 2
    rows4 = rows * steps
    pieces = 2 * ctx
    stacked = STACK * rows4
    smem = pl.BlockSpec(memory_space=pltpu.SMEM)
    vmem = pl.BlockSpec(memory_space=pltpu.VMEM)
    hbm = pl.BlockSpec(memory_space=pl.ANY)
    dma = pltpu.SemaphoreType.DMA
    flops = 4 * rows4 * width * (tokens * ctx + rows4)
    out = pl.pallas_call(
        functools.partial(kernel, (ctx, steps, cap, kv_heads, per_key)),
        out_shape=jax.ShapeDtypeStruct((owners, cap * steps, width), jnp.bfloat16),
        in_specs=[smem, smem, smem, vmem, vmem, vmem, hbm, hbm],
        out_specs=hbm,
        scratch_shapes=[
            pltpu.VMEM((kv_heads, ctx, 2, 2, half, HEAD_SIZE), jnp.bfloat16),
            pltpu.VMEM((pieces, rows4, half), jnp.float32),
            pltpu.VMEM((rows4, rows4), jnp.float32),
            pltpu.VMEM((pieces, stacked, half), jnp.float32),
            pltpu.VMEM((stacked, rows4), jnp.float32),
            pltpu.VMEM((owners * cap * steps, rows4), jnp.bfloat16),
            pltpu.VMEM((kv_heads, owners, cap * steps, per_key * HEAD_SIZE), jnp.bfloat16),
            dma((kv_heads, 2, 2)),
            dma((kv_heads, ctx)),
            dma((kv_heads, ctx)),
            dma((kv_heads, ctx)),
            dma((kv_heads, ctx)),
            dma((kv_heads, ctx)),
            dma((kv_heads, owners)),
            dma((kv_heads, owners)),
            dma((kv_heads,)),
        ],
        compiler_params=pltpu.CompilerParams(
            collective_id=0, has_side_effects=True, vmem_limit_bytes=48 * 1024 * 1024
        ),
        cost_estimate=pl.CostEstimate(
            flops=flops, bytes_accessed=8 * 1024 * 1024, transcendentals=flops // 512
        ),
    )(
        row_len,
        home[:, 0],
        block_pages,
        queries.reshape(rows4, width),
        row_new_keys.reshape(rows4, -1),
        row_new_values.reshape(rows4, -1),
        prefix_page_keys,
        prefix_page_values,
    )
    return out.reshape(1, owners, cap, steps, width)


def solution(mesh):
    return jax.shard_map(
        body,
        mesh=mesh,
        in_specs=(
            P(("groups", "ctx", "row"), None, "head"),
            P(("groups", "ctx", "row"), None, "head"),
            P(("groups", "ctx", "row"), None, "head"),
            P(("groups", "ctx"), "head"),
            P(("groups", "ctx"), "head"),
            P("groups", None),
            P(("groups", "ctx", "row")),
            P(("groups", "ctx", "row"), None),
        ),
        out_specs=P(("groups", "ctx", "row"), None, None, None, "head"),
        check_vma=False,
    )
```

```python
import functools

import jax
import jax.numpy as jnp
from jax import lax
from jax.experimental import pallas as pl
from jax.experimental.pallas import tpu as pltpu
from jax.sharding import PartitionSpec as P

HEAD_SIZE = 128
PAGE_TOKENS = 128
BLOCK_ROWS = 8
VMEM_BYTES = 58 * 1024 * 1024
LOWEST = -1e30
STACK = 2
AHEAD = 2
MESH = pl.DeviceIdType.MESH


def kernel(
    dims,
    len_ref,
    home_ref,
    pages_ref,
    q_hbm,
    nk_hbm,
    nv_hbm,
    pk_ref,
    pv_ref,
    out_ref,
    q_ref,
    nk_ref,
    nv_ref,
    row_sem,
    q_flat,
    nk_flat,
    nv_flat,
    kv,
    bias,
    own_bias,
    scores,
    placing,
    outbox,
    load_sem,
    up_send,
    down_send,
    z_recv,
    mate_send,
    mate_recv,
    out_send,
    out_recv,
    own_sem,
):
    ctx, steps, cap, kv_heads, per_key = dims
    rows = q_ref.shape[0]
    rows4 = rows * steps
    owners = 2 * ctx
    half = kv.shape[4]
    slots = pages_ref.shape[0]
    pool = ctx * 2 * half // PAGE_TOKENS
    wide = per_key * HEAD_SIZE
    pieces = 2 * ctx
    c = lax.axis_index("ctx")
    r = lax.axis_index("row")
    me = c * 2 + r
    factor = HEAD_SIZE ** (-0.5)

    def load(j, h, which):
        source = (pk_ref, pv_ref)[which]
        return pltpu.make_async_copy(
            source.at[pl.ds(h * half, half), pl.ds(j * HEAD_SIZE, HEAD_SIZE)],
            kv.at[j, c, h, which],
            load_sem.at[j, h, which],
        )

    for j in range(kv_heads):
        for h in range(2):
            for which in range(2):
                load(j, h, which).start()
    own_rows = [
        pltpu.make_async_copy(source, target, row_sem.at[i])
        for i, (source, target) in enumerate(
            ((q_hbm, q_ref), (nk_hbm, nk_ref), (nv_hbm, nv_ref))
        )
    ]
    for copy in own_rows:
        copy.start()

    barrier = pltpu.get_barrier_semaphore()

    def greet(k, _):
        other = lax.rem(me + k, owners)
        pl.semaphore_signal(
            barrier,
            inc=1,
            device_id={"ctx": other // 2, "row": lax.rem(other, 2)},
            device_id_type=MESH,
        )
        return 0

    lax.fori_loop(1, owners, greet, 0)
    pl.semaphore_wait(barrier, owners - 1)

    def along(j, o, ahead):
        step = 1 if ahead else -1
        target = jnp.clip(c + step, 0, ctx - 1)
        return pltpu.make_async_remote_copy(
            src_ref=kv.at[j, o, r],
            dst_ref=kv.at[j, o, r],
            send_sem=(up_send if ahead else down_send).at[j, o],
            recv_sem=z_recv.at[j, o],
            device_id={"ctx": target, "row": r},
            device_id_type=MESH,
        )

    def across(j, o, h):
        return pltpu.make_async_remote_copy(
            src_ref=kv.at[j, o, h],
            dst_ref=kv.at[j, o, h],
            send_sem=mate_send.at[j, o],
            recv_sem=mate_recv.at[j, o],
            device_id={"ctx": c, "row": 1 - r},
            device_id_type=MESH,
        )

    def send_own(j):
        @pl.when(c < ctx - 1)
        def _():
            along(j, c, True).start()

        @pl.when(c > 0)
        def _():
            along(j, c, False).start()

    def relay(j, s):
        low, high = c - s, c + s

        @pl.when(low >= 0)
        def _():
            along(j, low, True).wait_recv()

            @pl.when(c < ctx - 1)
            def _():
                along(j, low, True).start()

            across(j, low, r).start()

        @pl.when(high < ctx)
        def _():
            along(j, high, False).wait_recv()

            @pl.when(c > 0)
            def _():
                along(j, high, False).start()

            across(j, high, r).start()

    def wait_mate(j):
        def one(k, _):
            o = lax.rem(c + k, ctx)
            across(j, o, 1 - r).wait_recv()
            return 0

        lax.fori_loop(1, ctx, one, 0)

    for j in range(kv_heads):
        for h in range(2):
            for which in range(2):
                load(j, h, which).wait()
        if j < AHEAD:
            send_own(j)
    relay(0, 1)

    row_of = lax.broadcasted_iota(jnp.int32, (rows4, 1), 0) // steps
    lane_row = lax.broadcasted_iota(jnp.int32, (1, rows4), 1) // steps
    lane_step = lax.rem(lax.broadcasted_iota(jnp.int32, (1, rows4), 1), steps)
    length = jnp.zeros((rows4, 1), jnp.int32)
    home_col = jnp.zeros((rows4, 1), jnp.int32)
    home_lane = jnp.zeros((1, rows4), jnp.int32)
    for i in range(rows):
        length = jnp.where(row_of == i, len_ref[i], length)
        home_col = jnp.where(row_of == i, home_ref[i], home_col)
        home_lane = jnp.where(lane_row == i, home_ref[i], home_lane)

    page_id = lax.broadcasted_iota(jnp.int32, (rows4, pool), 1)
    used = jnp.zeros((rows4, pool), jnp.float32)
    block_of = row_of // BLOCK_ROWS
    first_block = me * (rows // BLOCK_ROWS)
    for slot in range(slots):
        page = jnp.zeros((rows4, 1), jnp.int32)
        for b in range(rows // BLOCK_ROWS):
            page = jnp.where(block_of == b, pages_ref[slot, first_block + b], page)
        page = jnp.where(slot < length, page, -1)
        used = jnp.where(page_id == page, 1.0, used)
    floor = jnp.where(used > 0.5, 0.0, LOWEST)
    per_piece = half // PAGE_TOKENS
    for p in range(pool):
        at = (p % per_piece) * PAGE_TOKENS
        bias[p // per_piece, :, at : at + PAGE_TOKENS] = jnp.broadcast_to(
            floor[:, p : p + 1], (rows4, PAGE_TOKENS)
        )
    row_step = lax.rem(lax.broadcasted_iota(jnp.int32, (rows4, 1), 0), steps)
    own_bias[...] = jnp.where((row_of == lane_row) & (lane_step <= row_step), 0.0, LOWEST)

    earlier = (home_col == home_lane) & (row_of < lane_row) & (row_step == 0)
    position = jnp.sum(jnp.where(earlier, 1.0, 0.0), axis=0, keepdims=True).astype(jnp.int32)
    target = (home_lane * cap + position) * steps + lane_step
    slot_row = lax.broadcasted_iota(jnp.int32, (owners * cap * steps, rows4), 0)
    placing[...] = jnp.where(slot_row == target, 1.0, 0.0).astype(jnp.bfloat16)

    def flatten(source, target, h):
        at = pl.multiple_of(h * HEAD_SIZE, HEAD_SIZE)
        got = source[:, :, pl.ds(at, HEAD_SIZE)].astype(jnp.float32)
        target[h] = got.reshape(rows4, HEAD_SIZE).astype(jnp.bfloat16)

    for copy in own_rows:
        copy.wait()

    def flatten_queries(h, _):
        flatten(q_ref, q_flat, h)
        return 0

    lax.fori_loop(0, kv_heads * per_key, flatten_queries, 0)
    for j in range(kv_heads):
        flatten(nk_ref, nk_flat, j)
        flatten(nv_ref, nv_flat, j)

    def first(s, _):
        relay(0, s)
        return 0

    lax.fori_loop(2, ctx, first, 0)

    chunks = per_key // STACK
    relays = -(-(ctx - 1) // chunks)
    contract = (((1,), (1,)), ((), ()))

    def over_pieces(step, init):
        if pieces <= 8:
            state = init
            for i in range(pieces):
                state = step(i, i // 2, i % 2, state)
            return state
        return lax.fori_loop(0, pieces, lambda i, st: step(i, i // 2, lax.rem(i, 2), st), init)

    def fold(op, array):
        got = array[:, :HEAD_SIZE]
        for at in range(HEAD_SIZE, array.shape[1], HEAD_SIZE):
            got = op(got, array[:, at : at + HEAD_SIZE])
        return got

    def send_result(j, o):
        return pltpu.make_async_remote_copy(
            src_ref=outbox.at[j, o],
            dst_ref=out_ref.at[me, :, pl.ds(pl.multiple_of(j * wide, wide), wide)],
            send_sem=out_send.at[j, o],
            recv_sem=out_recv.at[j, me],
            device_id={"ctx": o // 2, "row": lax.rem(o, 2)},
            device_id_type=MESH,
        )

    def take_result(j, o):
        return pltpu.make_async_remote_copy(
            src_ref=outbox.at[j, o],
            dst_ref=out_ref.at[o, :, pl.ds(pl.multiple_of(j * wide, wide), wide)],
            send_sem=out_send.at[j, o],
            recv_sem=out_recv.at[j, o],
            device_id={"ctx": o // 2, "row": lax.rem(o, 2)},
            device_id_type=MESH,
        )

    def keep_result(j):
        return pltpu.make_async_copy(
            outbox.at[j, me],
            out_ref.at[me, :, pl.ds(pl.multiple_of(j * wide, wide), wide)],
            own_sem.at[j],
        )

    def one_head(j, _):
        @pl.when(j + AHEAD < kv_heads)
        def _():
            send_own(j + AHEAD)

        wait_mate(j)

        def one_chunk(k, _):
            @pl.when(j + 1 < kv_heads)
            def _():
                for i in range(relays):
                    s = k * relays + i + 1

                    @pl.when(s < ctx)
                    def _():
                        relay(j + 1, s)

            lead = j * per_key + k * STACK
            query = q_flat[pl.ds(lead, STACK)].reshape(STACK * rows4, HEAD_SIZE)
            own = (
                lax.dot_general(
                    query,
                    nk_flat[j],
                    contract,
                    preferred_element_type=jnp.float32,
                )
                * factor
                + jnp.concatenate([own_bias[...]] * STACK, axis=0)
            )

            def score(i, o, h, peak):
                got = (
                    lax.dot_general(
                        query, kv[j, o, h, 0], contract, preferred_element_type=jnp.float32
                    )
                    * factor
                    + jnp.concatenate([bias[i]] * STACK, axis=0)
                )
                scores[i] = got
                return jnp.maximum(peak, fold(jnp.maximum, got))

            peak = jnp.max(over_pieces(score, own), axis=1, keepdims=True)
            weight = jnp.exp(own - peak)
            total = weight
            summed = jnp.dot(
                weight.astype(jnp.bfloat16),
                nv_flat[j],
                preferred_element_type=jnp.float32,
            )

            def gather(i, o, h, state):
                total, summed = state
                weight = jnp.exp(scores[i] - peak)
                summed = summed + jnp.dot(
                    weight.astype(jnp.bfloat16), kv[j, o, h, 1], preferred_element_type=jnp.float32
                )
                return total + fold(jnp.add, weight), summed

            total, summed = over_pieces(gather, (total, summed))
            attended = (summed / jnp.sum(total, axis=1, keepdims=True)).astype(jnp.bfloat16)
            for g in range(STACK):
                placed = jnp.dot(
                    placing[...],
                    attended[g * rows4 : (g + 1) * rows4],
                    preferred_element_type=jnp.float32,
                )
                at = pl.multiple_of((k * STACK + g) * HEAD_SIZE, HEAD_SIZE)
                outbox[j, :, :, pl.ds(at, HEAD_SIZE)] = placed.reshape(
                    owners, cap * steps, HEAD_SIZE
                ).astype(jnp.bfloat16)
            return 0

        lax.fori_loop(0, chunks, one_chunk, 0)

        def deliver(i, inner, k, _):
            o = lax.rem(me + k, owners)
            place = o // 2
            middle = (place >= (ctx + 2) // 4) & (place < ctx - (ctx + 2) // 4)

            @pl.when(middle if inner else ~middle)
            def _():
                send_result(i, o).start()

            return 0

        keep_result(j).start()
        lax.fori_loop(1, owners, functools.partial(deliver, j, True), 0)

        @pl.when(j >= kv_heads - 2)
        def _():
            def late(i, _):
                return lax.fori_loop(1, owners, functools.partial(deliver, i, False), 0)

            lax.fori_loop(jnp.where(j == kv_heads - 1, j, 0), j + 1, late, 0)

        return 0

    lax.fori_loop(0, kv_heads, one_head, 0)

    def settle(j, _):
        keep_result(j).wait()

        def pages(k, _):
            o = lax.rem(c + k, ctx)
            across(j, o, r).wait_send()
            return 0

        lax.fori_loop(1, ctx, pages, 0)

        def hops(o, _):
            @pl.when((c < ctx - 1) & (o <= c))
            def _():
                along(j, o, True).wait_send()

            @pl.when((c > 0) & (o >= c))
            def _():
                along(j, o, False).wait_send()

            return 0

        lax.fori_loop(0, ctx, hops, 0)

        def results(k, _):
            o = lax.rem(me + k, owners)
            send_result(j, o).wait_send()
            take_result(j, o).wait_recv()
            return 0

        lax.fori_loop(1, owners, results, 0)
        return 0

    lax.fori_loop(0, kv_heads, settle, 0)


def body(
    queries,
    row_new_keys,
    row_new_values,
    prefix_page_keys,
    prefix_page_values,
    block_pages,
    row_len,
    home,
):
    rows, steps, width = queries.shape
    kv_heads = row_new_keys.shape[2] // HEAD_SIZE
    per_key = width // row_new_keys.shape[2]
    ctx = lax.axis_size("ctx")
    owners = ctx * lax.axis_size("row")
    cap = max(2, 2 * rows // owners)
    tokens = prefix_page_keys.shape[0]
    half = tokens // 2
    rows4 = rows * steps
    pieces = 2 * ctx
    stacked = STACK * rows4
    smem = pl.BlockSpec(memory_space=pltpu.SMEM)
    hbm = pl.BlockSpec(memory_space=pl.ANY)
    dma = pltpu.SemaphoreType.DMA
    flops = 4 * rows4 * width * (tokens * ctx + rows4)
    out = pl.pallas_call(
        functools.partial(kernel, (ctx, steps, cap, kv_heads, per_key)),
        out_shape=jax.ShapeDtypeStruct((owners, cap * steps, width), jnp.bfloat16),
        in_specs=[smem, smem, smem, hbm, hbm, hbm, hbm, hbm],
        out_specs=hbm,
        scratch_shapes=[
            pltpu.VMEM(queries.shape, jnp.bfloat16),
            pltpu.VMEM(row_new_keys.shape, jnp.bfloat16),
            pltpu.VMEM(row_new_values.shape, jnp.bfloat16),
            dma((3,)),
            pltpu.VMEM((kv_heads * per_key, rows4, HEAD_SIZE), jnp.bfloat16),
            pltpu.VMEM((kv_heads, rows4, HEAD_SIZE), jnp.bfloat16),
            pltpu.VMEM((kv_heads, rows4, HEAD_SIZE), jnp.bfloat16),
            pltpu.VMEM((kv_heads, ctx, 2, 2, half, HEAD_SIZE), jnp.bfloat16),
            pltpu.VMEM((pieces, rows4, half), jnp.float32),
            pltpu.VMEM((rows4, rows4), jnp.float32),
            pltpu.VMEM((pieces, stacked, half), jnp.float32),
            pltpu.VMEM((owners * cap * steps, rows4), jnp.bfloat16),
            pltpu.VMEM((kv_heads, owners, cap * steps, per_key * HEAD_SIZE), jnp.bfloat16),
            dma((kv_heads, 2, 2)),
            dma((kv_heads, ctx)),
            dma((kv_heads, ctx)),
            dma((kv_heads, ctx)),
            dma((kv_heads, ctx)),
            dma((kv_heads, ctx)),
            dma((kv_heads, owners)),
            dma((kv_heads, owners)),
            dma((kv_heads,)),
        ],
        compiler_params=pltpu.CompilerParams(
            collective_id=0, has_side_effects=True, vmem_limit_bytes=VMEM_BYTES
        ),
        cost_estimate=pl.CostEstimate(
            flops=flops, bytes_accessed=8 * 1024 * 1024, transcendentals=flops // 512
        ),
    )(
        row_len,
        home[:, 0],
        block_pages.T,
        queries,
        row_new_keys,
        row_new_values,
        prefix_page_keys,
        prefix_page_values,
    )
    return out.reshape(1, owners, cap, steps, width)


def solution(mesh):
    return jax.shard_map(
        body,
        mesh=mesh,
        in_specs=(
            P(("groups", "ctx", "row"), None, "head"),
            P(("groups", "ctx", "row"), None, "head"),
            P(("groups", "ctx", "row"), None, "head"),
            P(("groups", "ctx"), "head"),
            P(("groups", "ctx"), "head"),
            P("groups", None),
            P(("groups", "ctx", "row")),
            P(("groups", "ctx", "row"), None),
        ),
        out_specs=P(("groups", "ctx", "row"), None, None, None, "head"),
        check_vma=False,
    )
```

```python
import functools

import jax
import jax.numpy as jnp
from jax import lax
from jax.experimental import pallas as pl
from jax.experimental.pallas import tpu as pltpu
from jax.sharding import PartitionSpec as P

HEAD_SIZE = 128
PAGE_TOKENS = 128
BLOCK_ROWS = 8
VMEM_BYTES = 58 * 1024 * 1024
LOWEST = -1e30
PASSED = 2
STACK = 4
AHEAD = 3
MESH = pl.DeviceIdType.MESH


def kernel(
    dims,
    len_ref,
    home_ref,
    pages_ref,
    q_hbm,
    nk_hbm,
    nv_hbm,
    pk_ref,
    pv_ref,
    out_ref,
    q_ref,
    nk_ref,
    nv_ref,
    row_sem,
    q_flat,
    nk_flat,
    nv_flat,
    kv,
    bias,
    own_bias,
    scores,
    placing,
    outbox,
    load_sem,
    up_send,
    down_send,
    z_recv,
    mate_send,
    mate_recv,
    out_send,
    out_recv,
    own_sem,
):
    ctx, steps, cap, kv_heads, per_key = dims
    rows = q_ref.shape[0]
    rows4 = rows * steps
    owners = 2 * ctx
    half = kv.shape[4]
    slots = pages_ref.shape[0]
    pool = ctx * 2 * half // PAGE_TOKENS
    wide = per_key * HEAD_SIZE
    pieces = 2 * ctx
    c = lax.axis_index("ctx")
    r = lax.axis_index("row")
    me = c * 2 + r
    factor = HEAD_SIZE ** (-0.5)

    def load(j, h, which):
        source = (pk_ref, pv_ref)[which]
        return pltpu.make_async_copy(
            source.at[pl.ds(h * half, half), pl.ds(j * HEAD_SIZE, HEAD_SIZE)],
            kv.at[j, c, h, which],
            load_sem.at[j, h, which],
        )

    for j in range(kv_heads):
        for h in range(2):
            for which in range(2):
                load(j, h, which).start()
    own_rows = [
        pltpu.make_async_copy(source, target, row_sem.at[i])
        for i, (source, target) in enumerate(
            ((q_hbm, q_ref), (nk_hbm, nk_ref), (nv_hbm, nv_ref))
        )
    ]
    for copy in own_rows:
        copy.start()

    barrier = pltpu.get_barrier_semaphore()

    def greet(k, _):
        other = lax.rem(me + k, owners)
        pl.semaphore_signal(
            barrier,
            inc=1,
            device_id={"ctx": other // 2, "row": lax.rem(other, 2)},
            device_id_type=MESH,
        )
        return 0

    lax.fori_loop(1, owners, greet, 0)
    pl.semaphore_wait(barrier, owners - 1)

    def along(j, o, ahead):
        step = 1 if ahead else -1
        target = jnp.clip(c + step, 0, ctx - 1)
        return pltpu.make_async_remote_copy(
            src_ref=kv.at[j, o, r],
            dst_ref=kv.at[j, o, r],
            send_sem=(up_send if ahead else down_send).at[j, o],
            recv_sem=z_recv.at[j, o],
            device_id={"ctx": target, "row": r},
            device_id_type=MESH,
        )

    def across(j, o, h):
        return pltpu.make_async_remote_copy(
            src_ref=kv.at[j, o, h],
            dst_ref=kv.at[j, o, h],
            send_sem=mate_send.at[j, o],
            recv_sem=mate_recv.at[j, o],
            device_id={"ctx": c, "row": 1 - r},
            device_id_type=MESH,
        )

    def send_own(j):
        @pl.when(c < ctx - 1)
        def _():
            along(j, c, True).start()

        @pl.when(c > 0)
        def _():
            along(j, c, False).start()

    def relay(j, s):
        low, high = c - s, c + s

        @pl.when(low >= 0)
        def _():
            along(j, low, True).wait_recv()

            @pl.when(c < ctx - 1)
            def _():
                along(j, low, True).start()

            across(j, low, r).start()

        @pl.when(high < ctx)
        def _():
            along(j, high, False).wait_recv()

            @pl.when(c > 0)
            def _():
                along(j, high, False).start()

            across(j, high, r).start()

    def wait_mate(j):
        def one(k, _):
            o = lax.rem(c + k, ctx)
            across(j, o, 1 - r).wait_recv()
            return 0

        lax.fori_loop(1, ctx, one, 0)

    for j in range(kv_heads):
        for h in range(2):
            for which in range(2):
                load(j, h, which).wait()
        if j < PASSED:
            send_own(j)

    row_of = lax.broadcasted_iota(jnp.int32, (rows4, 1), 0) // steps
    lane_row = lax.broadcasted_iota(jnp.int32, (1, rows4), 1) // steps
    lane_step = lax.rem(lax.broadcasted_iota(jnp.int32, (1, rows4), 1), steps)
    length = jnp.zeros((rows4, 1), jnp.int32)
    home_col = jnp.zeros((rows4, 1), jnp.int32)
    home_lane = jnp.zeros((1, rows4), jnp.int32)
    for i in range(rows):
        length = jnp.where(row_of == i, len_ref[i], length)
        home_col = jnp.where(row_of == i, home_ref[i], home_col)
        home_lane = jnp.where(lane_row == i, home_ref[i], home_lane)

    page_id = lax.broadcasted_iota(jnp.int32, (rows4, pool), 1)
    used = jnp.zeros((rows4, pool), jnp.float32)
    block_of = row_of // BLOCK_ROWS
    first_block = me * (rows // BLOCK_ROWS)
    for slot in range(slots):
        page = jnp.zeros((rows4, 1), jnp.int32)
        for b in range(rows // BLOCK_ROWS):
            page = jnp.where(block_of == b, pages_ref[slot, first_block + b], page)
        page = jnp.where(slot < length, page, -1)
        used = jnp.where(page_id == page, 1.0, used)
    floor = jnp.where(used > 0.5, 0.0, LOWEST)
    per_piece = half // PAGE_TOKENS
    for p in range(pool):
        at = (p % per_piece) * PAGE_TOKENS
        bias[p // per_piece, :, at : at + PAGE_TOKENS] = jnp.broadcast_to(
            floor[:, p : p + 1], (rows4, PAGE_TOKENS)
        )
    row_step = lax.rem(lax.broadcasted_iota(jnp.int32, (rows4, 1), 0), steps)
    own_bias[...] = jnp.where((row_of == lane_row) & (lane_step <= row_step), 0.0, LOWEST)

    earlier = (home_col == home_lane) & (row_of < lane_row) & (row_step == 0)
    position = jnp.sum(jnp.where(earlier, 1.0, 0.0), axis=0, keepdims=True).astype(jnp.int32)
    target = (home_lane * cap + position) * steps + lane_step
    slot_row = lax.broadcasted_iota(jnp.int32, (owners * cap * steps, rows4), 0)
    placing[...] = jnp.where(slot_row == target, 1.0, 0.0).astype(jnp.bfloat16)

    relay(0, 1)
    for j in range(PASSED, AHEAD):
        send_own(j)
    for j in range(1, PASSED):
        relay(j, 1)

    def flatten(source, target, h):
        at = pl.multiple_of(h * HEAD_SIZE, HEAD_SIZE)
        got = source[:, :, pl.ds(at, HEAD_SIZE)].astype(jnp.float32)
        target[h] = got.reshape(rows4, HEAD_SIZE).astype(jnp.bfloat16)

    for copy in own_rows:
        copy.wait()

    def flatten_queries(h, _):
        flatten(q_ref, q_flat, h)
        return 0

    lax.fori_loop(0, kv_heads * per_key, flatten_queries, 0)
    for j in range(kv_heads):
        flatten(nk_ref, nk_flat, j)
        flatten(nv_ref, nv_flat, j)

    def first(s, _):
        for j in range(PASSED):
            relay(j, s)
        return 0

    lax.fori_loop(2, ctx, first, 0)

    chunks = per_key // STACK
    relays = -(-(ctx - 1) // (2 * chunks))
    contract = (((1,), (1,)), ((), ()))

    def over_pieces(step, init):
        if pieces <= 8:
            state = init
            for i in range(pieces):
                state = step(i, i // 2, i % 2, state)
            return state
        return lax.fori_loop(0, pieces, lambda i, st: step(i, i // 2, lax.rem(i, 2), st), init)

    def fold(op, array):
        got = array[:, :HEAD_SIZE]
        for at in range(HEAD_SIZE, array.shape[1], HEAD_SIZE):
            got = op(got, array[:, at : at + HEAD_SIZE])
        return got

    def send_result(j, o):
        return pltpu.make_async_remote_copy(
            src_ref=outbox.at[j, o],
            dst_ref=out_ref.at[me, :, pl.ds(pl.multiple_of(j * wide, wide), wide)],
            send_sem=out_send.at[j, o],
            recv_sem=out_recv.at[j, me],
            device_id={"ctx": o // 2, "row": lax.rem(o, 2)},
            device_id_type=MESH,
        )

    def take_result(j, o):
        return pltpu.make_async_remote_copy(
            src_ref=outbox.at[j, o],
            dst_ref=out_ref.at[o, :, pl.ds(pl.multiple_of(j * wide, wide), wide)],
            send_sem=out_send.at[j, o],
            recv_sem=out_recv.at[j, o],
            device_id={"ctx": o // 2, "row": lax.rem(o, 2)},
            device_id_type=MESH,
        )

    def keep_result(j):
        return pltpu.make_async_copy(
            outbox.at[j, me],
            out_ref.at[me, :, pl.ds(pl.multiple_of(j * wide, wide), wide)],
            own_sem.at[j],
        )

    def one_head(j, _):
        @pl.when(j + AHEAD < kv_heads)
        def _():
            send_own(j + AHEAD)

        wait_mate(j)

        def one_chunk(k, _):
            def pass_on(turn):
                @pl.when(j + PASSED < kv_heads)
                def _():
                    for i in range(relays):
                        s = turn * relays + i + 1

                        @pl.when(s < ctx)
                        def _():
                            relay(j + PASSED, s)

            pass_on(2 * k)
            lead = j * per_key + k * STACK
            query = q_flat[pl.ds(lead, STACK)].reshape(STACK * rows4, HEAD_SIZE)
            own = (
                lax.dot_general(
                    query,
                    nk_flat[j],
                    contract,
                    preferred_element_type=jnp.float32,
                )
                * factor
                + jnp.concatenate([own_bias[...]] * STACK, axis=0)
            )

            def score(i, o, h, peak):
                got = (
                    lax.dot_general(
                        query, kv[j, o, h, 0], contract, preferred_element_type=jnp.float32
                    )
                    * factor
                    + jnp.concatenate([bias[i]] * STACK, axis=0)
                )
                scores[i] = got
                return jnp.maximum(peak, fold(jnp.maximum, got))

            peak = jnp.max(over_pieces(score, own), axis=1, keepdims=True)
            pass_on(2 * k + 1)
            weight = jnp.exp(own - peak)
            total = weight
            summed = jnp.dot(
                weight.astype(jnp.bfloat16),
                nv_flat[j],
                preferred_element_type=jnp.float32,
            )

            def gather(i, o, h, state):
                total, summed = state
                weight = jnp.exp(scores[i] - peak)
                summed = summed + jnp.dot(
                    weight.astype(jnp.bfloat16), kv[j, o, h, 1], preferred_element_type=jnp.float32
                )
                return total + fold(jnp.add, weight), summed

            total, summed = over_pieces(gather, (total, summed))
            attended = (summed / jnp.sum(total, axis=1, keepdims=True)).astype(jnp.bfloat16)
            for g in range(STACK):
                placed = jnp.dot(
                    placing[...],
                    attended[g * rows4 : (g + 1) * rows4],
                    preferred_element_type=jnp.float32,
                )
                at = pl.multiple_of((k * STACK + g) * HEAD_SIZE, HEAD_SIZE)
                outbox[j, :, :, pl.ds(at, HEAD_SIZE)] = placed.reshape(
                    owners, cap * steps, HEAD_SIZE
                ).astype(jnp.bfloat16)
            return 0

        lax.fori_loop(0, chunks, one_chunk, 0)

        def deliver(k, _):
            send_result(j, lax.rem(me + k, owners)).start()
            return 0

        lax.fori_loop(1, owners, deliver, 0)
        keep_result(j).start()
        return 0

    lax.fori_loop(0, kv_heads, one_head, 0)

    def settle(j, _):
        keep_result(j).wait()

        def pages(k, _):
            o = lax.rem(c + k, ctx)
            across(j, o, r).wait_send()
            return 0

        lax.fori_loop(1, ctx, pages, 0)

        def hops(o, _):
            @pl.when((c < ctx - 1) & (o <= c))
            def _():
                along(j, o, True).wait_send()

            @pl.when((c > 0) & (o >= c))
            def _():
                along(j, o, False).wait_send()

            return 0

        lax.fori_loop(0, ctx, hops, 0)

        def results(k, _):
            o = lax.rem(me + k, owners)
            send_result(j, o).wait_send()
            take_result(j, o).wait_recv()
            return 0

        lax.fori_loop(1, owners, results, 0)
        return 0

    lax.fori_loop(0, kv_heads, settle, 0)


def body(
    queries,
    row_new_keys,
    row_new_values,
    prefix_page_keys,
    prefix_page_values,
    block_pages,
    row_len,
    home,
):
    rows, steps, width = queries.shape
    kv_heads = row_new_keys.shape[2] // HEAD_SIZE
    per_key = width // row_new_keys.shape[2]
    ctx = lax.axis_size("ctx")
    owners = ctx * lax.axis_size("row")
    cap = max(2, 2 * rows // owners)
    tokens = prefix_page_keys.shape[0]
    half = tokens // 2
    rows4 = rows * steps
    pieces = 2 * ctx
    stacked = STACK * rows4
    smem = pl.BlockSpec(memory_space=pltpu.SMEM)
    hbm = pl.BlockSpec(memory_space=pl.ANY)
    dma = pltpu.SemaphoreType.DMA
    flops = 4 * rows4 * width * (tokens * ctx + rows4)
    out = pl.pallas_call(
        functools.partial(kernel, (ctx, steps, cap, kv_heads, per_key)),
        out_shape=jax.ShapeDtypeStruct((owners, cap * steps, width), jnp.bfloat16),
        in_specs=[smem, smem, smem, hbm, hbm, hbm, hbm, hbm],
        out_specs=hbm,
        scratch_shapes=[
            pltpu.VMEM(queries.shape, jnp.bfloat16),
            pltpu.VMEM(row_new_keys.shape, jnp.bfloat16),
            pltpu.VMEM(row_new_values.shape, jnp.bfloat16),
            dma((3,)),
            pltpu.VMEM((kv_heads * per_key, rows4, HEAD_SIZE), jnp.bfloat16),
            pltpu.VMEM((kv_heads, rows4, HEAD_SIZE), jnp.bfloat16),
            pltpu.VMEM((kv_heads, rows4, HEAD_SIZE), jnp.bfloat16),
            pltpu.VMEM((kv_heads, ctx, 2, 2, half, HEAD_SIZE), jnp.bfloat16),
            pltpu.VMEM((pieces, rows4, half), jnp.float32),
            pltpu.VMEM((rows4, rows4), jnp.float32),
            pltpu.VMEM((pieces, stacked, half), jnp.float32),
            pltpu.VMEM((owners * cap * steps, rows4), jnp.bfloat16),
            pltpu.VMEM((kv_heads, owners, cap * steps, per_key * HEAD_SIZE), jnp.bfloat16),
            dma((kv_heads, 2, 2)),
            dma((kv_heads, ctx)),
            dma((kv_heads, ctx)),
            dma((kv_heads, ctx)),
            dma((kv_heads, ctx)),
            dma((kv_heads, ctx)),
            dma((kv_heads, owners)),
            dma((kv_heads, owners)),
            dma((kv_heads,)),
        ],
        compiler_params=pltpu.CompilerParams(
            collective_id=0, has_side_effects=True, vmem_limit_bytes=VMEM_BYTES
        ),
        cost_estimate=pl.CostEstimate(
            flops=flops, bytes_accessed=8 * 1024 * 1024, transcendentals=flops // 512
        ),
    )(
        row_len,
        home[:, 0],
        block_pages.T,
        queries,
        row_new_keys,
        row_new_values,
        prefix_page_keys,
        prefix_page_values,
    )
    return out.reshape(1, owners, cap, steps, width)


def solution(mesh):
    return jax.shard_map(
        body,
        mesh=mesh,
        in_specs=(
            P(("groups", "ctx", "row"), None, "head"),
            P(("groups", "ctx", "row"), None, "head"),
            P(("groups", "ctx", "row"), None, "head"),
            P(("groups", "ctx"), "head"),
            P(("groups", "ctx"), "head"),
            P("groups", None),
            P(("groups", "ctx", "row")),
            P(("groups", "ctx", "row"), None),
        ),
        out_specs=P(("groups", "ctx", "row"), None, None, None, "head"),
        check_vma=False,
    )
```

```python
import functools

import jax
import jax.numpy as jnp
from jax import lax
from jax.experimental import pallas as pl
from jax.experimental.pallas import tpu as pltpu
from jax.sharding import PartitionSpec as P

HEAD_SIZE = 128
PAGE_TOKENS = 128
BLOCK_ROWS = 8
VMEM_BYTES = 58 * 1024 * 1024
LOWEST = -1e30
PASSED = 2
STACK = 4
AHEAD = 3
MESH = pl.DeviceIdType.MESH


def kernel(
    dims,
    len_ref,
    home_ref,
    pages_ref,
    q_hbm,
    nk_hbm,
    nv_hbm,
    pk_ref,
    pv_ref,
    out_ref,
    q_ref,
    nk_ref,
    nv_ref,
    row_sem,
    q_flat,
    nk_flat,
    nv_flat,
    kv,
    bias,
    own_bias,
    scores,
    placing,
    outbox,
    load_sem,
    up_send,
    down_send,
    z_recv,
    mate_send,
    mate_recv,
    out_send,
    out_recv,
    own_sem,
):
    ctx, steps, cap, kv_heads, per_key = dims
    rows = q_ref.shape[0]
    rows4 = rows * steps
    owners = 2 * ctx
    half = kv.shape[4]
    slots = pages_ref.shape[0]
    pool = ctx * 2 * half // PAGE_TOKENS
    wide = STACK * HEAD_SIZE
    pieces = 2 * ctx
    c = lax.axis_index("ctx")
    r = lax.axis_index("row")
    me = c * 2 + r
    factor = HEAD_SIZE ** (-0.5)

    def load(j, h, which):
        source = (pk_ref, pv_ref)[which]
        return pltpu.make_async_copy(
            source.at[pl.ds(h * half, half), pl.ds(j * HEAD_SIZE, HEAD_SIZE)],
            kv.at[j, c, h, which],
            load_sem.at[j, h, which],
        )

    for j in range(kv_heads):
        for h in range(2):
            for which in range(2):
                load(j, h, which).start()
    own_rows = [
        pltpu.make_async_copy(source, target, row_sem.at[i])
        for i, (source, target) in enumerate(
            ((q_hbm, q_ref), (nk_hbm, nk_ref), (nv_hbm, nv_ref))
        )
    ]
    for copy in own_rows:
        copy.start()

    barrier = pltpu.get_barrier_semaphore()

    def greet(k, _):
        other = lax.rem(me + k, owners)
        pl.semaphore_signal(
            barrier,
            inc=1,
            device_id={"ctx": other // 2, "row": lax.rem(other, 2)},
            device_id_type=MESH,
        )
        return 0

    lax.fori_loop(1, owners, greet, 0)
    pl.semaphore_wait(barrier, owners - 1)

    def along(j, o, ahead):
        step = 1 if ahead else -1
        target = jnp.clip(c + step, 0, ctx - 1)
        return pltpu.make_async_remote_copy(
            src_ref=kv.at[j, o, r],
            dst_ref=kv.at[j, o, r],
            send_sem=(up_send if ahead else down_send).at[j, o],
            recv_sem=z_recv.at[j, o],
            device_id={"ctx": target, "row": r},
            device_id_type=MESH,
        )

    def across(j, o, h):
        return pltpu.make_async_remote_copy(
            src_ref=kv.at[j, o, h],
            dst_ref=kv.at[j, o, h],
            send_sem=mate_send.at[j, o],
            recv_sem=mate_recv.at[j, o],
            device_id={"ctx": c, "row": 1 - r},
            device_id_type=MESH,
        )

    def send_own(j):
        @pl.when(c < ctx - 1)
        def _():
            along(j, c, True).start()

        @pl.when(c > 0)
        def _():
            along(j, c, False).start()

    def relay(j, s):
        low, high = c - s, c + s

        @pl.when(low >= 0)
        def _():
            along(j, low, True).wait_recv()

            @pl.when(c < ctx - 1)
            def _():
                along(j, low, True).start()

            across(j, low, r).start()

        @pl.when(high < ctx)
        def _():
            along(j, high, False).wait_recv()

            @pl.when(c > 0)
            def _():
                along(j, high, False).start()

            across(j, high, r).start()

    def wait_mate(j):
        def one(k, _):
            o = lax.rem(c + k, ctx)
            across(j, o, 1 - r).wait_recv()
            return 0

        lax.fori_loop(1, ctx, one, 0)

    for j in range(kv_heads):
        for h in range(2):
            for which in range(2):
                load(j, h, which).wait()
        if j < PASSED:
            send_own(j)

    row_of = lax.broadcasted_iota(jnp.int32, (rows4, 1), 0) // steps
    lane_row = lax.broadcasted_iota(jnp.int32, (1, rows4), 1) // steps
    lane_step = lax.rem(lax.broadcasted_iota(jnp.int32, (1, rows4), 1), steps)
    length = jnp.zeros((rows4, 1), jnp.int32)
    home_col = jnp.zeros((rows4, 1), jnp.int32)
    home_lane = jnp.zeros((1, rows4), jnp.int32)
    for i in range(rows):
        length = jnp.where(row_of == i, len_ref[i], length)
        home_col = jnp.where(row_of == i, home_ref[i], home_col)
        home_lane = jnp.where(lane_row == i, home_ref[i], home_lane)

    page_id = lax.broadcasted_iota(jnp.int32, (rows4, pool), 1)
    used = jnp.zeros((rows4, pool), jnp.float32)
    block_of = row_of // BLOCK_ROWS
    first_block = me * (rows // BLOCK_ROWS)
    for slot in range(slots):
        page = jnp.zeros((rows4, 1), jnp.int32)
        for b in range(rows // BLOCK_ROWS):
            page = jnp.where(block_of == b, pages_ref[slot, first_block + b], page)
        page = jnp.where(slot < length, page, -1)
        used = jnp.where(page_id == page, 1.0, used)
    floor = jnp.where(used > 0.5, 0.0, LOWEST)
    per_piece = half // PAGE_TOKENS
    for p in range(pool):
        at = (p % per_piece) * PAGE_TOKENS
        bias[p // per_piece, :, at : at + PAGE_TOKENS] = jnp.broadcast_to(
            floor[:, p : p + 1], (rows4, PAGE_TOKENS)
        )
    row_step = lax.rem(lax.broadcasted_iota(jnp.int32, (rows4, 1), 0), steps)
    own_bias[...] = jnp.where((row_of == lane_row) & (lane_step <= row_step), 0.0, LOWEST)

    earlier = (home_col == home_lane) & (row_of < lane_row) & (row_step == 0)
    position = jnp.sum(jnp.where(earlier, 1.0, 0.0), axis=0, keepdims=True).astype(jnp.int32)
    target = (home_lane * cap + position) * steps + lane_step
    slot_row = lax.broadcasted_iota(jnp.int32, (owners * cap * steps, rows4), 0)
    placing[...] = jnp.where(slot_row == target, 1.0, 0.0).astype(jnp.bfloat16)

    relay(0, 1)
    for j in range(PASSED, AHEAD):
        send_own(j)
    for j in range(1, PASSED):
        relay(j, 1)

    def flatten(source, target, h):
        at = pl.multiple_of(h * HEAD_SIZE, HEAD_SIZE)
        got = source[:, :, pl.ds(at, HEAD_SIZE)].astype(jnp.float32)
        target[h] = got.reshape(rows4, HEAD_SIZE).astype(jnp.bfloat16)

    for copy in own_rows:
        copy.wait()

    def flatten_queries(h, _):
        flatten(q_ref, q_flat, h)
        return 0

    lax.fori_loop(0, kv_heads * per_key, flatten_queries, 0)
    for j in range(kv_heads):
        flatten(nk_ref, nk_flat, j)
        flatten(nv_ref, nv_flat, j)

    def first(s, _):
        for j in range(PASSED):
            relay(j, s)
        return 0

    lax.fori_loop(2, ctx, first, 0)

    chunks = per_key // STACK
    relays = -(-(ctx - 1) // (2 * chunks))
    contract = (((1,), (1,)), ((), ()))

    def over_pieces(step, init):
        if pieces <= 8:
            state = init
            for i in range(pieces):
                state = step(i, i // 2, i % 2, state)
            return state
        return lax.fori_loop(0, pieces, lambda i, st: step(i, i // 2, lax.rem(i, 2), st), init)

    def fold(op, array):
        got = array[:, :HEAD_SIZE]
        for at in range(HEAD_SIZE, array.shape[1], HEAD_SIZE):
            got = op(got, array[:, at : at + HEAD_SIZE])
        return got

    def send_result(j, o):
        return pltpu.make_async_remote_copy(
            src_ref=outbox.at[j, o],
            dst_ref=out_ref.at[me, :, pl.ds(pl.multiple_of(j * wide, wide), wide)],
            send_sem=out_send.at[j, o],
            recv_sem=out_recv.at[j, me],
            device_id={"ctx": o // 2, "row": lax.rem(o, 2)},
            device_id_type=MESH,
        )

    def take_result(j, o):
        return pltpu.make_async_remote_copy(
            src_ref=outbox.at[j, o],
            dst_ref=out_ref.at[o, :, pl.ds(pl.multiple_of(j * wide, wide), wide)],
            send_sem=out_send.at[j, o],
            recv_sem=out_recv.at[j, o],
            device_id={"ctx": o // 2, "row": lax.rem(o, 2)},
            device_id_type=MESH,
        )

    def keep_result(j):
        return pltpu.make_async_copy(
            outbox.at[j, me],
            out_ref.at[me, :, pl.ds(pl.multiple_of(j * wide, wide), wide)],
            own_sem.at[j],
        )

    def one_head(j, _):
        @pl.when(j + AHEAD < kv_heads)
        def _():
            send_own(j + AHEAD)

        wait_mate(j)

        def one_chunk(k, _):
            def pass_on(turn):
                @pl.when(j + PASSED < kv_heads)
                def _():
                    for i in range(relays):
                        s = turn * relays + i + 1

                        @pl.when(s < ctx)
                        def _():
                            relay(j + PASSED, s)

            pass_on(2 * k)
            lead = j * per_key + k * STACK
            query = q_flat[pl.ds(lead, STACK)].reshape(STACK * rows4, HEAD_SIZE)
            own = (
                lax.dot_general(
                    query,
                    nk_flat[j],
                    contract,
                    preferred_element_type=jnp.float32,
                )
                * factor
                + jnp.concatenate([own_bias[...]] * STACK, axis=0)
            )

            def score(i, o, h, peak):
                got = (
                    lax.dot_general(
                        query, kv[j, o, h, 0], contract, preferred_element_type=jnp.float32
                    )
                    * factor
                    + jnp.concatenate([bias[i]] * STACK, axis=0)
                )
                scores[i] = got
                return jnp.maximum(peak, fold(jnp.maximum, got))

            peak = jnp.max(over_pieces(score, own), axis=1, keepdims=True)
            pass_on(2 * k + 1)
            weight = jnp.exp(own - peak)
            total = weight
            summed = jnp.dot(
                weight.astype(jnp.bfloat16),
                nv_flat[j],
                preferred_element_type=jnp.float32,
            )

            def gather(i, o, h, state):
                total, summed = state
                weight = jnp.exp(scores[i] - peak)
                summed = summed + jnp.dot(
                    weight.astype(jnp.bfloat16), kv[j, o, h, 1], preferred_element_type=jnp.float32
                )
                return total + fold(jnp.add, weight), summed

            total, summed = over_pieces(gather, (total, summed))
            attended = (summed / jnp.sum(total, axis=1, keepdims=True)).astype(jnp.bfloat16)
            part = j * chunks + k
            for g in range(STACK):
                placed = jnp.dot(
                    placing[...],
                    attended[g * rows4 : (g + 1) * rows4],
                    preferred_element_type=jnp.float32,
                )
                outbox[part, :, :, g * HEAD_SIZE : (g + 1) * HEAD_SIZE] = placed.reshape(
                    owners, cap * steps, HEAD_SIZE
                ).astype(jnp.bfloat16)

            def deliver(i, _):
                send_result(part, lax.rem(me + i, owners)).start()
                return 0

            lax.fori_loop(1, owners, deliver, 0)
            keep_result(part).start()
            return 0

        lax.fori_loop(0, chunks, one_chunk, 0)
        return 0

    lax.fori_loop(0, kv_heads, one_head, 0)

    def settle(j, _):
        def pages(k, _):
            o = lax.rem(c + k, ctx)
            across(j, o, r).wait_send()
            return 0

        lax.fori_loop(1, ctx, pages, 0)

        def hops(o, _):
            @pl.when((c < ctx - 1) & (o <= c))
            def _():
                along(j, o, True).wait_send()

            @pl.when((c > 0) & (o >= c))
            def _():
                along(j, o, False).wait_send()

            return 0

        lax.fori_loop(0, ctx, hops, 0)

        return 0

    def settle_part(part, _):
        keep_result(part).wait()

        def results(k, _):
            o = lax.rem(me + k, owners)
            send_result(part, o).wait_send()
            take_result(part, o).wait_recv()
            return 0

        lax.fori_loop(1, owners, results, 0)
        return 0

    lax.fori_loop(0, kv_heads, settle, 0)
    lax.fori_loop(0, kv_heads * chunks, settle_part, 0)


def body(
    queries,
    row_new_keys,
    row_new_values,
    prefix_page_keys,
    prefix_page_values,
    block_pages,
    row_len,
    home,
):
    rows, steps, width = queries.shape
    kv_heads = row_new_keys.shape[2] // HEAD_SIZE
    per_key = width // row_new_keys.shape[2]
    ctx = lax.axis_size("ctx")
    owners = ctx * lax.axis_size("row")
    cap = max(2, 2 * rows // owners)
    tokens = prefix_page_keys.shape[0]
    half = tokens // 2
    rows4 = rows * steps
    parts = kv_heads * (per_key // STACK)
    pieces = 2 * ctx
    stacked = STACK * rows4
    smem = pl.BlockSpec(memory_space=pltpu.SMEM)
    hbm = pl.BlockSpec(memory_space=pl.ANY)
    dma = pltpu.SemaphoreType.DMA
    flops = 4 * rows4 * width * (tokens * ctx + rows4)
    out = pl.pallas_call(
        functools.partial(kernel, (ctx, steps, cap, kv_heads, per_key)),
        out_shape=jax.ShapeDtypeStruct((owners, cap * steps, width), jnp.bfloat16),
        in_specs=[smem, smem, smem, hbm, hbm, hbm, hbm, hbm],
        out_specs=hbm,
        scratch_shapes=[
            pltpu.VMEM(queries.shape, jnp.bfloat16),
            pltpu.VMEM(row_new_keys.shape, jnp.bfloat16),
            pltpu.VMEM(row_new_values.shape, jnp.bfloat16),
            dma((3,)),
            pltpu.VMEM((kv_heads * per_key, rows4, HEAD_SIZE), jnp.bfloat16),
            pltpu.VMEM((kv_heads, rows4, HEAD_SIZE), jnp.bfloat16),
            pltpu.VMEM((kv_heads, rows4, HEAD_SIZE), jnp.bfloat16),
            pltpu.VMEM((kv_heads, ctx, 2, 2, half, HEAD_SIZE), jnp.bfloat16),
            pltpu.VMEM((pieces, rows4, half), jnp.float32),
            pltpu.VMEM((rows4, rows4), jnp.float32),
            pltpu.VMEM((pieces, stacked, half), jnp.float32),
            pltpu.VMEM((owners * cap * steps, rows4), jnp.bfloat16),
            pltpu.VMEM((parts, owners, cap * steps, STACK * HEAD_SIZE), jnp.bfloat16),
            dma((kv_heads, 2, 2)),
            dma((kv_heads, ctx)),
            dma((kv_heads, ctx)),
            dma((kv_heads, ctx)),
            dma((kv_heads, ctx)),
            dma((kv_heads, ctx)),
            dma((parts, owners)),
            dma((parts, owners)),
            dma((parts,)),
        ],
        compiler_params=pltpu.CompilerParams(
            collective_id=0, has_side_effects=True, vmem_limit_bytes=VMEM_BYTES
        ),
        cost_estimate=pl.CostEstimate(
            flops=flops, bytes_accessed=8 * 1024 * 1024, transcendentals=flops // 512
        ),
    )(
        row_len,
        home[:, 0],
        block_pages.T,
        queries,
        row_new_keys,
        row_new_values,
        prefix_page_keys,
        prefix_page_values,
    )
    return out.reshape(1, owners, cap, steps, width)


def solution(mesh):
    return jax.shard_map(
        body,
        mesh=mesh,
        in_specs=(
            P(("groups", "ctx", "row"), None, "head"),
            P(("groups", "ctx", "row"), None, "head"),
            P(("groups", "ctx", "row"), None, "head"),
            P(("groups", "ctx"), "head"),
            P(("groups", "ctx"), "head"),
            P("groups", None),
            P(("groups", "ctx", "row")),
            P(("groups", "ctx", "row"), None),
        ),
        out_specs=P(("groups", "ctx", "row"), None, None, None, "head"),
        check_vma=False,
    )
```

```python
import functools

import jax
import jax.numpy as jnp
from jax import lax
from jax.experimental import pallas as pl
from jax.experimental.pallas import tpu as pltpu
from jax.sharding import PartitionSpec as P

HEAD_SIZE = 128
PAGE_TOKENS = 128
BLOCK_ROWS = 8
VMEM_BYTES = 58 * 1024 * 1024
LOWEST = -1e30
PASSED = 2
STACK = 2
AHEAD = 3
MESH = pl.DeviceIdType.MESH


def kernel(
    dims,
    len_ref,
    home_ref,
    pages_ref,
    q_hbm,
    nk_hbm,
    nv_hbm,
    pk_ref,
    pv_ref,
    out_ref,
    q_ref,
    nk_ref,
    nv_ref,
    row_sem,
    q_flat,
    nk_flat,
    nv_flat,
    kv,
    bias,
    own_bias,
    scores,
    placing,
    outbox,
    load_sem,
    up_send,
    down_send,
    z_recv,
    mate_send,
    mate_recv,
    out_send,
    out_recv,
    own_sem,
):
    ctx, steps, cap, kv_heads, per_key = dims
    rows = q_ref.shape[0]
    rows4 = rows * steps
    owners = 2 * ctx
    half = kv.shape[4]
    slots = pages_ref.shape[0]
    pool = ctx * 2 * half // PAGE_TOKENS
    wide = STACK * HEAD_SIZE
    pieces = 2 * ctx
    c = lax.axis_index("ctx")
    r = lax.axis_index("row")
    me = c * 2 + r
    factor = HEAD_SIZE ** (-0.5)

    def load(j, h, which):
        source = (pk_ref, pv_ref)[which]
        return pltpu.make_async_copy(
            source.at[pl.ds(h * half, half), pl.ds(j * HEAD_SIZE, HEAD_SIZE)],
            kv.at[j, c, h, which],
            load_sem.at[j, h, which],
        )

    for j in range(kv_heads):
        for h in range(2):
            for which in range(2):
                load(j, h, which).start()
    own_rows = [
        pltpu.make_async_copy(source, target, row_sem.at[i])
        for i, (source, target) in enumerate(
            ((q_hbm, q_ref), (nk_hbm, nk_ref), (nv_hbm, nv_ref))
        )
    ]
    for copy in own_rows:
        copy.start()

    barrier = pltpu.get_barrier_semaphore()

    def greet(k, _):
        other = lax.rem(me + k, owners)
        pl.semaphore_signal(
            barrier,
            inc=1,
            device_id={"ctx": other // 2, "row": lax.rem(other, 2)},
            device_id_type=MESH,
        )
        return 0

    lax.fori_loop(1, owners, greet, 0)
    pl.semaphore_wait(barrier, owners - 1)

    def along(j, o, ahead):
        step = 1 if ahead else -1
        target = jnp.clip(c + step, 0, ctx - 1)
        return pltpu.make_async_remote_copy(
            src_ref=kv.at[j, o, r],
            dst_ref=kv.at[j, o, r],
            send_sem=(up_send if ahead else down_send).at[j, o],
            recv_sem=z_recv.at[j, o],
            device_id={"ctx": target, "row": r},
            device_id_type=MESH,
        )

    def across(j, o, h):
        return pltpu.make_async_remote_copy(
            src_ref=kv.at[j, o, h],
            dst_ref=kv.at[j, o, h],
            send_sem=mate_send.at[j, o],
            recv_sem=mate_recv.at[j, o],
            device_id={"ctx": c, "row": 1 - r},
            device_id_type=MESH,
        )

    def send_own(j):
        @pl.when(c < ctx - 1)
        def _():
            along(j, c, True).start()

        @pl.when(c > 0)
        def _():
            along(j, c, False).start()

    def relay(j, s):
        low, high = c - s, c + s

        @pl.when(low >= 0)
        def _():
            along(j, low, True).wait_recv()

            @pl.when(c < ctx - 1)
            def _():
                along(j, low, True).start()

            across(j, low, r).start()

        @pl.when(high < ctx)
        def _():
            along(j, high, False).wait_recv()

            @pl.when(c > 0)
            def _():
                along(j, high, False).start()

            across(j, high, r).start()

    def wait_mate(j):
        def one(k, _):
            o = lax.rem(c + k, ctx)
            across(j, o, 1 - r).wait_recv()
            return 0

        lax.fori_loop(1, ctx, one, 0)

    for j in range(kv_heads):
        for h in range(2):
            for which in range(2):
                load(j, h, which).wait()
        if j < PASSED:
            send_own(j)

    row_of = lax.broadcasted_iota(jnp.int32, (rows4, 1), 0) // steps
    lane_row = lax.broadcasted_iota(jnp.int32, (1, rows4), 1) // steps
    lane_step = lax.rem(lax.broadcasted_iota(jnp.int32, (1, rows4), 1), steps)
    length = jnp.zeros((rows4, 1), jnp.int32)
    home_col = jnp.zeros((rows4, 1), jnp.int32)
    home_lane = jnp.zeros((1, rows4), jnp.int32)
    for i in range(rows):
        length = jnp.where(row_of == i, len_ref[i], length)
        home_col = jnp.where(row_of == i, home_ref[i], home_col)
        home_lane = jnp.where(lane_row == i, home_ref[i], home_lane)

    page_id = lax.broadcasted_iota(jnp.int32, (rows4, pool), 1)
    used = jnp.zeros((rows4, pool), jnp.float32)
    block_of = row_of // BLOCK_ROWS
    first_block = me * (rows // BLOCK_ROWS)
    for slot in range(slots):
        page = jnp.zeros((rows4, 1), jnp.int32)
        for b in range(rows // BLOCK_ROWS):
            page = jnp.where(block_of == b, pages_ref[slot, first_block + b], page)
        page = jnp.where(slot < length, page, -1)
        used = jnp.where(page_id == page, 1.0, used)
    floor = jnp.where(used > 0.5, 0.0, LOWEST)
    per_piece = half // PAGE_TOKENS
    for p in range(pool):
        at = (p % per_piece) * PAGE_TOKENS
        bias[p // per_piece, :, at : at + PAGE_TOKENS] = jnp.broadcast_to(
            floor[:, p : p + 1], (rows4, PAGE_TOKENS)
        )
    row_step = lax.rem(lax.broadcasted_iota(jnp.int32, (rows4, 1), 0), steps)
    own_bias[...] = jnp.where((row_of == lane_row) & (lane_step <= row_step), 0.0, LOWEST)

    earlier = (home_col == home_lane) & (row_of < lane_row) & (row_step == 0)
    position = jnp.sum(jnp.where(earlier, 1.0, 0.0), axis=0, keepdims=True).astype(jnp.int32)
    target = (home_lane * cap + position) * steps + lane_step
    slot_row = lax.broadcasted_iota(jnp.int32, (owners * cap * steps, rows4), 0)
    placing[...] = jnp.where(slot_row == target, 1.0, 0.0).astype(jnp.bfloat16)

    relay(0, 1)
    for j in range(PASSED, AHEAD):
        send_own(j)
    for j in range(1, PASSED):
        relay(j, 1)

    def flatten(source, target, h):
        at = pl.multiple_of(h * HEAD_SIZE, HEAD_SIZE)
        got = source[:, :, pl.ds(at, HEAD_SIZE)].astype(jnp.float32)
        target[h] = got.reshape(rows4, HEAD_SIZE).astype(jnp.bfloat16)

    for copy in own_rows:
        copy.wait()

    def flatten_queries(h, _):
        flatten(q_ref, q_flat, h)
        return 0

    lax.fori_loop(0, kv_heads * per_key, flatten_queries, 0)
    for j in range(kv_heads):
        flatten(nk_ref, nk_flat, j)
        flatten(nv_ref, nv_flat, j)

    def first(s, _):
        for j in range(PASSED):
            relay(j, s)
        return 0

    lax.fori_loop(2, ctx, first, 0)

    chunks = per_key // STACK
    relays = -(-(ctx - 1) // (2 * chunks))
    contract = (((1,), (1,)), ((), ()))

    def over_pieces(step, init):
        if pieces <= 8:
            state = init
            for i in range(pieces):
                state = step(i, i // 2, i % 2, state)
            return state
        return lax.fori_loop(0, pieces, lambda i, st: step(i, i // 2, lax.rem(i, 2), st), init)

    def fold(op, array):
        got = array[:, :HEAD_SIZE]
        for at in range(HEAD_SIZE, array.shape[1], HEAD_SIZE):
            got = op(got, array[:, at : at + HEAD_SIZE])
        return got

    def send_result(j, o):
        return pltpu.make_async_remote_copy(
            src_ref=outbox.at[j, o],
            dst_ref=out_ref.at[me, :, pl.ds(pl.multiple_of(j * wide, wide), wide)],
            send_sem=out_send.at[j, o],
            recv_sem=out_recv.at[j, me],
            device_id={"ctx": o // 2, "row": lax.rem(o, 2)},
            device_id_type=MESH,
        )

    def take_result(j, o):
        return pltpu.make_async_remote_copy(
            src_ref=outbox.at[j, o],
            dst_ref=out_ref.at[o, :, pl.ds(pl.multiple_of(j * wide, wide), wide)],
            send_sem=out_send.at[j, o],
            recv_sem=out_recv.at[j, o],
            device_id={"ctx": o // 2, "row": lax.rem(o, 2)},
            device_id_type=MESH,
        )

    def keep_result(j):
        return pltpu.make_async_copy(
            outbox.at[j, me],
            out_ref.at[me, :, pl.ds(pl.multiple_of(j * wide, wide), wide)],
            own_sem.at[j],
        )

    def one_head(j, _):
        @pl.when(j + AHEAD < kv_heads)
        def _():
            send_own(j + AHEAD)

        wait_mate(j)

        def one_chunk(k, _):
            def pass_on(turn):
                @pl.when(j + PASSED < kv_heads)
                def _():
                    for i in range(relays):
                        s = turn * relays + i + 1

                        @pl.when(s < ctx)
                        def _():
                            relay(j + PASSED, s)

            pass_on(2 * k)
            lead = j * per_key + k * STACK
            query = q_flat[pl.ds(lead, STACK)].reshape(STACK * rows4, HEAD_SIZE)
            own = (
                lax.dot_general(
                    query,
                    nk_flat[j],
                    contract,
                    preferred_element_type=jnp.float32,
                )
                * factor
                + jnp.concatenate([own_bias[...]] * STACK, axis=0)
            )

            def score(i, o, h, peak):
                got = (
                    lax.dot_general(
                        query, kv[j, o, h, 0], contract, preferred_element_type=jnp.float32
                    )
                    * factor
                    + jnp.concatenate([bias[i]] * STACK, axis=0)
                )
                scores[i] = got
                return jnp.maximum(peak, fold(jnp.maximum, got))

            peak = jnp.max(over_pieces(score, own), axis=1, keepdims=True)
            pass_on(2 * k + 1)
            weight = jnp.exp(own - peak)
            total = weight
            summed = jnp.dot(
                weight.astype(jnp.bfloat16),
                nv_flat[j],
                preferred_element_type=jnp.float32,
            )

            def gather(i, o, h, state):
                total, summed = state
                weight = jnp.exp(scores[i] - peak)
                summed = summed + jnp.dot(
                    weight.astype(jnp.bfloat16), kv[j, o, h, 1], preferred_element_type=jnp.float32
                )
                return total + fold(jnp.add, weight), summed

            total, summed = over_pieces(gather, (total, summed))
            attended = (summed / jnp.sum(total, axis=1, keepdims=True)).astype(jnp.bfloat16)
            part = j * chunks + k
            for g in range(STACK):
                placed = jnp.dot(
                    placing[...],
                    attended[g * rows4 : (g + 1) * rows4],
                    preferred_element_type=jnp.float32,
                )
                outbox[part, :, :, g * HEAD_SIZE : (g + 1) * HEAD_SIZE] = placed.reshape(
                    owners, cap * steps, HEAD_SIZE
                ).astype(jnp.bfloat16)

            def deliver(i, _):
                send_result(part, lax.rem(me + i, owners)).start()
                return 0

            lax.fori_loop(1, owners, deliver, 0)
            keep_result(part).start()
            return 0

        lax.fori_loop(0, chunks, one_chunk, 0)
        return 0

    lax.fori_loop(0, kv_heads, one_head, 0)

    def settle(j, _):
        def pages(k, _):
            o = lax.rem(c + k, ctx)
            across(j, o, r).wait_send()
            return 0

        lax.fori_loop(1, ctx, pages, 0)

        def hops(o, _):
            @pl.when((c < ctx - 1) & (o <= c))
            def _():
                along(j, o, True).wait_send()

            @pl.when((c > 0) & (o >= c))
            def _():
                along(j, o, False).wait_send()

            return 0

        lax.fori_loop(0, ctx, hops, 0)

        return 0

    def settle_part(part, _):
        keep_result(part).wait()

        def results(k, _):
            o = lax.rem(me + k, owners)
            send_result(part, o).wait_send()
            take_result(part, o).wait_recv()
            return 0

        lax.fori_loop(1, owners, results, 0)
        return 0

    lax.fori_loop(0, kv_heads, settle, 0)
    lax.fori_loop(0, kv_heads * chunks, settle_part, 0)


def body(
    queries,
    row_new_keys,
    row_new_values,
    prefix_page_keys,
    prefix_page_values,
    block_pages,
    row_len,
    home,
):
    rows, steps, width = queries.shape
    kv_heads = row_new_keys.shape[2] // HEAD_SIZE
    per_key = width // row_new_keys.shape[2]
    ctx = lax.axis_size("ctx")
    owners = ctx * lax.axis_size("row")
    cap = max(2, 2 * rows // owners)
    tokens = prefix_page_keys.shape[0]
    half = tokens // 2
    rows4 = rows * steps
    parts = kv_heads * (per_key // STACK)
    pieces = 2 * ctx
    stacked = STACK * rows4
    smem = pl.BlockSpec(memory_space=pltpu.SMEM)
    hbm = pl.BlockSpec(memory_space=pl.ANY)
    dma = pltpu.SemaphoreType.DMA
    flops = 4 * rows4 * width * (tokens * ctx + rows4)
    out = pl.pallas_call(
        functools.partial(kernel, (ctx, steps, cap, kv_heads, per_key)),
        out_shape=jax.ShapeDtypeStruct((owners, cap * steps, width), jnp.bfloat16),
        in_specs=[smem, smem, smem, hbm, hbm, hbm, hbm, hbm],
        out_specs=hbm,
        scratch_shapes=[
            pltpu.VMEM(queries.shape, jnp.bfloat16),
            pltpu.VMEM(row_new_keys.shape, jnp.bfloat16),
            pltpu.VMEM(row_new_values.shape, jnp.bfloat16),
            dma((3,)),
            pltpu.VMEM((kv_heads * per_key, rows4, HEAD_SIZE), jnp.bfloat16),
            pltpu.VMEM((kv_heads, rows4, HEAD_SIZE), jnp.bfloat16),
            pltpu.VMEM((kv_heads, rows4, HEAD_SIZE), jnp.bfloat16),
            pltpu.VMEM((kv_heads, ctx, 2, 2, half, HEAD_SIZE), jnp.bfloat16),
            pltpu.VMEM((pieces, rows4, half), jnp.float32),
            pltpu.VMEM((rows4, rows4), jnp.float32),
            pltpu.VMEM((pieces, stacked, half), jnp.float32),
            pltpu.VMEM((owners * cap * steps, rows4), jnp.bfloat16),
            pltpu.VMEM((parts, owners, cap * steps, STACK * HEAD_SIZE), jnp.bfloat16),
            dma((kv_heads, 2, 2)),
            dma((kv_heads, ctx)),
            dma((kv_heads, ctx)),
            dma((kv_heads, ctx)),
            dma((kv_heads, ctx)),
            dma((kv_heads, ctx)),
            dma((parts, owners)),
            dma((parts, owners)),
            dma((parts,)),
        ],
        compiler_params=pltpu.CompilerParams(
            collective_id=0, has_side_effects=True, vmem_limit_bytes=VMEM_BYTES
        ),
        cost_estimate=pl.CostEstimate(
            flops=flops, bytes_accessed=8 * 1024 * 1024, transcendentals=flops // 512
        ),
    )(
        row_len,
        home[:, 0],
        block_pages.T,
        queries,
        row_new_keys,
        row_new_values,
        prefix_page_keys,
        prefix_page_values,
    )
    return out.reshape(1, owners, cap, steps, width)


def solution(mesh):
    return jax.shard_map(
        body,
        mesh=mesh,
        in_specs=(
            P(("groups", "ctx", "row"), None, "head"),
            P(("groups", "ctx", "row"), None, "head"),
            P(("groups", "ctx", "row"), None, "head"),
            P(("groups", "ctx"), "head"),
            P(("groups", "ctx"), "head"),
            P("groups", None),
            P(("groups", "ctx", "row")),
            P(("groups", "ctx", "row"), None),
        ),
        out_specs=P(("groups", "ctx", "row"), None, None, None, "head"),
        check_vma=False,
    )
```
